512 devices in a mesh: dp: 128 (over z, y, core), rep: 4 (over x).
Axes of the slice: x: 4, y: 8, z: 8, core: 2. Of those that a mesh axis runs over, the one named last changes fastest.
Arguments:
- tokens: bfloat16 [8192, 2048], P(('dp', 'rep')), may hold values from -6 to 6
- norm_gain: float32 [2048], replicated, may hold values from 0.1 to 1.9
- expert_weights: bfloat16 [64, 2048, 2304], P(None, ('dp', 'rep')), may hold values from -0.125 to 0.125
- slot_expert: int32 [128], replicated, may hold values from 0 to 63, as said below
- pair_slots: int32 [8192, 8], P(('dp', 'rep')), may hold values from 0 to 127, all different within a row; in each aligned block of 16 rows (0 to 15, 16 to 31, ...) at most 2 rows name the same one
- combine_weights: float32 [8192, 8], P(('dp', 'rep')), may hold values from 0.25 to 2
Outputs:
- layer_out: bfloat16 [8192, 2048], P(('dp', 'rep'))
The draws below stay inside these ranges and needn't reach their ends.
Inputs may be any that keep to these rules, and one draw needn't show every extreme that they name: `slot_expert`: every one of the 64 experts is held by at least one slot. `pair_slots`: each row names 8 different slots; among the 16 rows of one device no slot is named by more than 2 rows.
All inputs are finite; a program needn't handle non-finite values.
Results may differ from the reference program's by a relative error of at most 0.0071.
Values may be sent and summed in bfloat16 or wider, within the bound.
A program may use at most 64 MiB of HBM per device.

```python
import math
import jax
import jax.numpy as jnp
import numpy as np
from jax import lax

D = 2048
F = 768
TOPK = 8
TOK_DEV = 16
SLOTS = 128
EXPERTS = 64
CAP = 2
TOKENS = 8192
N_DP = 128


def draw_slot_expert(key, part):
    first_key = jax.random.fold_in(key, 11)
    second_key = jax.random.fold_in(key, 23)
    third_key = jax.random.fold_in(key, 37)
    hot_count = max(1, EXPERTS // 4)
    favoured = jax.random.permutation(first_key, EXPERTS)[:hot_count].astype(jnp.int32)
    extras = favoured[jax.random.randint(second_key, (SLOTS - EXPERTS,), 0, hot_count)]
    listing = jnp.concatenate([jnp.arange(EXPERTS, dtype=jnp.int32), extras.astype(jnp.int32)])
    return listing[jax.random.permutation(third_key, SLOTS)].astype(jnp.int32)


def block_scale(rng, extent, pieces, least, high):
    level = 1.0
    for axis_at, blocks in pieces:
        draws = jax.random.uniform(jax.random.fold_in(jax.random.fold_in(rng, 6), axis_at), (blocks,), jnp.float32, least / len(pieces), high / len(pieces))
        level = level * jnp.repeat(jnp.exp(draws), extent[axis_at] // blocks).reshape((-1,) + (1,) * (len(extent) - 1 - axis_at))
    return level


def assign_block(key, own, number, rows, count, top, bound, skew):
    order = jax.random.permutation(key, count)
    heavy_load, usual = portions_of(count, rows * top, bound, skew, True), portions_of(count, rows * top, bound, skew, False)
    places = jnp.arange(count)

    def named(sizes, rotation):
        used = int((sizes > 0).sum())
        fixed = max(1, used // 4)
        shifted = fixed + (places - fixed + rotation * (used - fixed)) % max(1, count - fixed)
        return jnp.zeros((count,), jnp.int32).at[order[jnp.where(places < fixed, places, shifted)]].set(jnp.asarray(sizes, jnp.int32))

    sizes = jnp.where(number % 4 == 0, named(heavy_load, number // 4), named(usual, number - number // 4 - 1))
    mixed = jax.random.permutation(jax.random.fold_in(own, 3), count)
    donor, receiver = mixed[0:count // 2 * 2:2], mixed[1:count // 2 * 2:2]
    room = jnp.minimum(sizes[donor] - 1, bound - sizes[receiver]) // 2
    room = jnp.where((donor == order[0]) | (receiver == order[0]) | (sizes[receiver] == 0), 0, jnp.maximum(room, 0))
    shifted = jax.random.randint(jax.random.fold_in(own, 4), (count // 2,), 0, 1 << 20) % (room + 1)
    sizes = sizes.at[donor].add(-shifted).at[receiver].add(shifted)
    labels = jnp.searchsorted(jnp.cumsum(sizes), jnp.arange(rows * top), side="right").astype(jnp.int32)
    table = labels.reshape(top, rows).T
    table = table[jax.random.permutation(jax.random.fold_in(own, 1), rows)]
    rotation = jax.random.randint(jax.random.fold_in(own, 2), (rows, 1), 0, top)
    return jnp.take_along_axis(table, (jnp.arange(top)[None, :] + rotation) % top, axis=1)


def portions_of(amount, total, limit, slope, full):
    portions = [(1 << 20) // math.isqrt(grade ** slope) + 1 for grade in range(1, amount + 1)]
    largest = limit if full else min(limit, max(-(-total // amount), total * portions[0] // sum(portions)))
    least = 1 if total - largest >= amount - 1 else 0
    given, surplus = [largest] + [least] * (amount - 1), total - largest - least * (amount - 1)
    while surplus > 0:
        free = [i for i in range(1, amount) if given[i] < largest] or [i for i in range(1, amount) if given[i] < limit]
        pool, budget = sum([portions[i] for i in free]), surplus
        for i in free:
            more = min(limit - given[i], max(1, budget * portions[i] // pool), surplus)
            given[i] = given[i] + more
            surplus = surplus - more
    return np.array(given)


def noise(stream_key, dims, spread, bound, pieces=(), kind=jnp.bfloat16):
    gain = block_scale(stream_key, dims, pieces, -0.22, 0.18) if pieces else 1.0
    array = jax.random.normal(stream_key, dims, jnp.float32) * spread * gain
    return jnp.minimum(jnp.maximum(array, -bound), bound).astype(kind)


def setup_inputs(seed: int = 0) -> dict:
    arg_keys = jax.random.split(jax.random.key(seed), 7)
    tokens = noise(arg_keys[0], (TOKENS, D), 1.0, 6.0, ((0, 512),))
    norm_gain = jnp.clip(1.0 + 0.18 * jax.random.normal(arg_keys[1], (D,), jnp.float32), 0.1, 1.9)
    expert_weights = noise(arg_keys[2], (EXPERTS, D, 3 * F), D ** -0.5, 0.125, ((1, 512),))
    slot_expert = draw_slot_expert(jax.random.fold_in(arg_keys[6], 71), 0)
    pair_slots_keys = jax.random.split(jax.random.fold_in(arg_keys[4], 1), TOKENS // TOK_DEV)
    pair_slots_turns = jax.random.permutation(jax.random.fold_in(arg_keys[4], 3), TOKENS // TOK_DEV)
    pair_slots = jax.vmap(lambda own, number: assign_block(jax.random.fold_in(arg_keys[4], 2), own, number, TOK_DEV, SLOTS, TOPK, CAP, 2))(pair_slots_keys, pair_slots_turns).reshape((TOKENS, TOPK))
    combine_weights = jnp.clip(jnp.exp(math.log(2.0) - 2.0794415 * jax.random.uniform(arg_keys[5], (TOKENS, TOPK), jnp.float32) ** block_scale(arg_keys[5], (TOKENS, TOPK), ((0, 512),), -0.2, 0.2)), 0.25, 2.0)
    return {"tokens": tokens, "norm_gain": norm_gain, "expert_weights": expert_weights, "slot_expert": slot_expert, "pair_slots": pair_slots, "combine_weights": combine_weights}


def reference(tokens, norm_gain, expert_weights, slot_expert, pair_slots, combine_weights):
    values = tokens.astype(jnp.float32)
    mean_square = lax.optimization_barrier(jnp.mean(values * values, axis=1, keepdims=True))
    normed = (values * lax.rsqrt(mean_square + 1e-06) * norm_gain[None, :]).astype(jnp.bfloat16)
    device_count = TOKENS // TOK_DEV
    pair_count = TOK_DEV * TOPK
    targets = pair_slots.reshape(device_count, pair_count).astype(jnp.int32)
    onehot = (targets[:, :, None] == jnp.arange(N_DP, dtype=jnp.int32)[None, None, :]).astype(jnp.int32)
    before = jnp.cumsum(onehot, axis=1) - onehot
    position = lax.optimization_barrier(jnp.sum(before * onehot, axis=2)).astype(jnp.int32)
    column = (jnp.arange(device_count, dtype=jnp.int32)[:, None] * CAP + position).astype(jnp.int32)
    pair_index = jnp.arange(device_count * pair_count, dtype=jnp.int32).reshape(device_count, pair_count)
    inverse = jnp.full((N_DP, device_count * CAP), -1, jnp.int32).at[targets, column].set(pair_index)

    def per_slot(inputs):
        slot_pairs, expert = inputs
        valid = slot_pairs >= 0
        token_rows = jnp.maximum(slot_pairs, 0) // TOPK
        rows = jnp.where(valid[:, None], normed[token_rows], jnp.zeros((), jnp.bfloat16))
        weight = expert_weights[expert]
        gate_up = jnp.dot(rows, weight[:, :2 * F], preferred_element_type=jnp.float32)
        hidden = (jax.nn.silu(gate_up[:, :F]) * gate_up[:, F:]).astype(jnp.bfloat16)
        return jnp.dot(hidden, weight[:, 2 * F:].T, preferred_element_type=jnp.float32).astype(jnp.bfloat16)
    outputs = lax.map(per_slot, (inverse, slot_expert.astype(jnp.int32)))
    expert_out = outputs[targets, column].astype(jnp.float32).reshape(TOKENS, TOPK, D)
    mixed = lax.optimization_barrier(jnp.sum(expert_out * combine_weights[:, :, None], axis=1))
    return mixed.astype(jnp.bfloat16)
```

```python
import jax
import jax.numpy as jnp
from jax import lax
from jax.experimental import pallas as pl
from jax.experimental.pallas import tpu as pltpu
from jax.sharding import PartitionSpec as P

NZ, NY, NX = 8, 8, 4
D, F, ROWS = 2048, 768, 16
HALF = D // 2
TILES = 3 * F // 128
BF16, F32 = jnp.bfloat16, jnp.float32


def mod(value, size):
    return lax.rem(value + 2 * size, size)


def kernel(tok_ref, gain_ref, w_ref, slot_ref, pair_ref, comb_ref, out_ref,
           xa, xb, wraw, wmat, acc, hid, coef, rs_send, rs_recv, fin_send, fin_recv,
           sem_a1, sem_b1, sem_s1, ring_r, ring_s, w_recv, w_send, w_own,
           x_recv, x_send, f_recv, f_send, c_recv, c_send,
           rs_r, rs_s, fin_r, fin_s):
    dp, x = lax.axis_index("dp"), lax.axis_index("rep")
    z, y, core = dp // (2 * NY), lax.rem(dp // 2, NY), lax.rem(dp, 2)

    def at(zz, yy):
        return (zz * (2 * NY) + yy * 2 + core, x)

    def move(src, dst, send, recv, device):
        return pltpu.make_async_remote_copy(
            src_ref=src, dst_ref=dst, send_sem=send, recv_sem=recv,
            device_id=device, device_id_type=pl.DeviceIdType.MESH)

    right, left = (dp, mod(x + 1, NX)), (dp, mod(x - 1, NX))
    other = (dp + 1 - 2 * core, x)

    barrier = pltpu.get_barrier_semaphore()

    def greet(i, _):
        pl.semaphore_signal(barrier, inc=1, device_id=at(mod(z + i // NY, NZ), mod(y + lax.rem(i, NY), NY)),
                            device_id_type=pl.DeviceIdType.MESH)
        return 0

    lax.fori_loop(1, NZ * NY, greet, 0)
    for device in (right, left, other):
        pl.semaphore_signal(barrier, inc=1, device_id=device, device_id_type=pl.DeviceIdType.MESH)

    values = tok_ref[...].astype(F32)
    mean_square = jnp.mean(values * values, axis=1, keepdims=True)
    normed = (values * lax.rsqrt(mean_square + 1e-06) * gain_ref[...]).astype(BF16)
    lane = lax.broadcasted_iota(jnp.int32, (ROWS, 128), 1)
    weights = jnp.zeros((ROWS, 128), F32)
    for k in range(8):
        held = jnp.sum(jnp.where(lane == pair_ref[:, k:k + 1], slot_ref[...], 0.0), axis=1, keepdims=True)
        weights = weights + jnp.where((lane & 63).astype(F32) == held, comb_ref[:, k:k + 1], 0.0)
    high = weights.astype(BF16)
    low = (weights - high.astype(F32)).astype(BF16)
    xa[z, y] = normed[:, :HALF]
    xb[y, z, :, :HALF] = normed[:, HALF:]
    xb[y, z, :, HALF:] = jnp.where(lane < 64, high.astype(F32), low.astype(F32)).astype(BF16)

    pl.semaphore_wait(barrier, NZ * NY + 2)

    def first_a(dy):
        return move(xa.at[z, y], xa.at[z, y], sem_s1.at[0], sem_a1, at(z, mod(y + dy, NY)))

    def first_b(dz):
        return move(xb.at[y, z], xb.at[y, z], sem_s1.at[1], sem_b1, at(mod(z + dz, NZ), y))

    def start_first(i, _):
        first_a(i).start()
        first_b(i).start()
        return 0

    lax.fori_loop(1, 8, start_first, 0)

    def offset(g):
        half = (g + 1) // 2
        odd = lax.rem(g, 2)
        return odd * half + (1 - odd) * lax.rem(NZ - half, NZ)

    own_w = pltpu.make_async_copy(w_ref.at[z * NY + y], wraw.at[core, x, z, y], w_own)
    own_w.start()

    def send_w(i, _):
        g, dy = i // NY, lax.rem(i, NY)
        zz, yy = mod(z + offset(g), NZ), mod(y + dy, NY)
        move(w_ref.at[zz * NY + yy], wraw.at[core, x, z, y], w_send, w_recv.at[g], at(zz, yy)).start()
        return 0

    lax.fori_loop(1, NZ * NY, send_w, 0)

    def block(half, index, part=None):
        ref = (xa, xb)[half]
        return ref.at[index] if part is None else ref.at[index, pl.ds(4 * part, 4)]

    def ring(half, way, step, part=None):
        sign = 1 - 2 * way
        mine = (z, y)[half]
        device = at(mod(z + sign, NZ), y) if half == 0 else at(z, mod(y + sign, NY))
        ref = block(half, mod(mine - sign * step, 8), part)
        index = (half * 2 + way) * 4 + step
        return move(ref, ref, ring_s.at[index], ring_r.at[index], device)

    def ring_landed(half, way, step, part=None):
        sign = 1 - 2 * way
        mine = (z, y)[half]
        ref = block(half, mod(mine - sign * (step + 1), 8), part)
        index = (half * 2 + way) * 4 + step
        move(ref, ref, ring_s.at[index], ring_r.at[index], right).wait_recv()

    def rows_step(step):
        if step == 0:
            move(xa.at[z, pl.ds(0, 7)], xa.at[z, pl.ds(0, 7)], sem_s1.at[0], sem_a1, right).wait_recv()
            move(xb.at[y, pl.ds(0, 7)], xb.at[y, pl.ds(0, 7)], sem_s1.at[1], sem_b1, right).wait_recv()
        for half in range(2):
            for way in range(2):
                if step > 0:
                    ring_landed(half, way, step - 1)
                ring(half, way, step, None if step < 3 else way).start()

    def rows_end():
        for half in range(2):
            for way in range(2):
                ring_landed(half, way, 3, way)
        mine = lax.broadcasted_iota(jnp.int32, (128, 128), 1) & 63
        mine = mine == z * NY + y

        def fill(i, _):
            for half in range(2):
                raw = xb[:, i, :, HALF:] if half == 0 else xb[i, :, :, HALF:]
                c = jnp.where(mine, raw.reshape(128, 128).astype(F32), 0.0)
                coef[half, i] = jnp.broadcast_to(jnp.sum(c, axis=1, keepdims=True), (128, 128))
            return 0

        lax.fori_loop(0, 8, fill, 0)

    acc[...] = jnp.zeros_like(acc)

    def multiply(g, _):
        zz = mod(z - offset(g), NZ)

        def tile(yy, _):
            for c in range(2):
                row = pl.multiple_of(yy * 32 + c * 16, 16)
                for t in range(TILES):
                    wmat[zz, pl.ds(row, 16), t * 128:(t + 1) * 128] = jnp.concatenate(
                        [wraw[c, i, zz, yy, t] for i in range(NX)], axis=0)
            return 0

        lax.fori_loop(0, NY, tile, 0)

        def add(rows_of, first):
            column = pl.multiple_of((zz - first) * 256, 256)

            def part(q, _):
                rows = rows_of(q, column)
                for n in range(3):
                    at_n = slice(n * 512, (n + 1) * 512)
                    spot = pl.ds(pl.multiple_of(q * 512, 512), 512)
                    acc[spot, at_n] += jnp.dot(rows, wmat[zz, :, at_n], preferred_element_type=F32)
                return 0

            lax.fori_loop(0, 2, part, 0)

        @pl.when(zz < 4)
        def _():
            add(lambda q, col: xa[pl.ds(q * 4, 4), :, :, pl.ds(col, 256)].reshape(512, 256), 0)

        @pl.when(zz >= 4)
        def _():
            add(lambda q, col: jnp.concatenate(
                [xb[:, q * 4 + i, :, pl.ds(col, 256)].reshape(128, 256) for i in range(4)], axis=0), 4)

        return 0

    def x_copy(g, way):
        zz = mod(z - offset(g), NZ)
        ref = wraw.at[core, x, zz]
        return move(ref, ref, x_send.at[way, g], x_recv.at[way, g], (right, left)[way])

    def x_forward(g, way):
        zz = mod(z - offset(g), NZ)
        ref = wraw.at[core, mod(x - 1 + 2 * way, NX), zz, pl.ds(4 * way, 4)]
        return move(ref, ref, f_send.at[way, g], f_recv.at[way, g], (right, left)[way])

    def core_copy(g):
        zz = mod(z - offset(g), NZ)
        ref = wraw.at[core, :, zz]
        return move(ref, ref, c_send.at[g], c_recv.at[g], other)

    def w_step(s, _):
        @pl.when(s < 8)
        def _():
            @pl.when(s == 0)
            def _():
                ref = wraw.at[core, x, z, pl.ds(0, 7)]
                move(ref, ref, w_send, w_recv.at[0], right).wait_recv()
                own_w.wait()

            @pl.when(s > 0)
            def _():
                ref = wraw.at[core, x, mod(z - offset(s), NZ)]
                move(ref, ref, w_send, w_recv.at[s], right).wait_recv()

            for way in range(2):
                x_copy(s, way).start()

        for i in range(4):
            pl.when(s == i)(lambda i=i: rows_step(i))
        pl.when(s == 4)(rows_end)

        @pl.when((s >= 1) & (s < 9))
        def _():
            for way in range(2):
                x_copy(s - 1, way).wait_recv()
                x_forward(s - 1, way).start()

        @pl.when((s >= 2) & (s < 10))
        def _():
            for way in range(2):
                x_forward(s - 2, way).wait_recv()
            core_copy(s - 2).start()

        @pl.when((s >= 3) & (s < 11))
        def _():
            core_copy(s - 3).wait_recv()

        @pl.when(s == 5)
        def _():
            lax.fori_loop(0, 3, multiply, 0)

        @pl.when(s > 5)
        def _():
            multiply(s - 3, 0)

        return 0

    lax.fori_loop(0, 11, w_step, 0)

    def activate(i, _):
        spot = pl.ds(pl.multiple_of(i * 128, 128), 128)
        gate, up = acc[spot, :F], acc[spot, F:]
        value = (gate / (1.0 + jnp.exp(-gate)) * up).astype(BF16).reshape(8, ROWS, F)
        hid[0, i] = value
        hid[1, :, i] = value
        return 0

    lax.fori_loop(0, 8, activate, 0)

    def term(half, index):
        rows = hid[half, index].reshape(128, F)
        scale = coef[half, index][:, :1]
        parts = [lax.dot_general(rows, wmat[half * 4 + i, :, 2 * F:], (((1,), (1,)), ((), ())),
                                 preferred_element_type=F32) for i in range(4)]
        return jnp.concatenate(parts, axis=1) * scale

    def beside(half, sign):
        return at(mod(z + (1 - half) * sign, NZ), mod(y + half * sign, NY))

    def mine_of(half):
        return (1 - half) * z + half * y

    def rs_first(half, way):
        ref = rs_send.at[half, way, 0, pl.ds(way * 64, 64)]
        dst = rs_recv.at[half, way, 0, pl.ds(way * 64, 64)]
        return move(ref, dst, rs_s.at[half, way, 0], rs_r.at[half, way, 0], beside(half, 1 - 2 * way))

    def rs_copy(half, way, step):
        return move(rs_send.at[half, way, step], rs_recv.at[half, way, step],
                    rs_s.at[half, way, step], rs_r.at[half, way, step], beside(half, 1 - 2 * way))

    def begin(half, _):
        value = term(half, mod(mine_of(half) + 4, 8)).astype(BF16)
        for way in range(2):
            rows = slice(way * 64, way * 64 + 64)
            rest = slice(64 - way * 64, 128 - way * 64)
            rs_send[half, way, 0, rows] = value[rows]
            rs_first(half, way).start()
            rs_recv[half, way, 0, rest] = jnp.zeros((64, HALF), BF16)
        return 0

    lax.fori_loop(0, 2, begin, 0)

    def go(i, _):
        step, half, way = 1 + i // 4, lax.rem(i // 2, 2), lax.rem(i, 2)
        sign = 1 - 2 * way
        value = term(half, mod(mine_of(half) + sign * (4 - step), 8))

        @pl.when(step == 1)
        def _():
            rs_first(half, way).wait_recv()

        @pl.when(step > 1)
        def _():
            rs_copy(half, way, step - 1).wait_recv()

        rs_send[half, way, step] = (value + rs_recv[half, way, step - 1].astype(F32)).astype(BF16)
        rs_copy(half, way, step).start()
        return 0

    def fin_copy(half, step):
        mine = (1 - half) * y + half * z
        there = mod(mine + step, 8)
        device = at((1 - half) * z + half * there, (1 - half) * there + half * y)
        return move(fin_send.at[half, there], fin_recv.at[half, mine], fin_s.at[half], fin_r.at[half], device)

    def end(half, _):
        value = term(half, mine_of(half))
        for way in range(2):
            rs_copy(half, way, 3).wait_recv()
            value = value + rs_recv[half, way, 3].astype(F32)
        value = value.astype(BF16).reshape(8, ROWS, HALF)
        fin_send[half] = value

        def spread(step, _):
            fin_copy(half, step).start()
            return 0

        lax.fori_loop(1, 8, spread, 0)
        mine = (1 - half) * y + half * z
        fin_recv[half, mine] = fin_send[half, mine]
        return 0

    lax.fori_loop(0, 12, go, 0)
    lax.fori_loop(0, 2, end, 0)

    for half in range(2):
        ref = fin_recv.at[half, pl.ds(0, 7)]
        move(ref, ref, fin_s.at[half], fin_r.at[half], right).wait_recv()
        total = fin_recv[half, 0].astype(F32)
        for i in range(1, 8):
            total = total + fin_recv[half, i].astype(F32)
        out_ref[:, half * HALF:(half + 1) * HALF] = total.astype(BF16)

    move(xa.at[z, pl.ds(0, 7)], xa.at[z, pl.ds(0, 7)], sem_s1.at[0], sem_a1, right).wait_send()
    move(xb.at[y, pl.ds(0, 7)], xb.at[y, pl.ds(0, 7)], sem_s1.at[1], sem_b1, right).wait_send()
    ref = w_ref.at[pl.ds(0, NZ * NY - 1)]
    move(ref, ref, w_send, w_recv.at[0], right).wait_send()
    for half in range(2):
        for way in range(2):
            for step in range(4):
                ring(half, way, step, None if step < 3 else way).wait_send()
            rs_first(half, way).wait_send()
            for step in range(1, 4):
                rs_copy(half, way, step).wait_send()
        ref = fin_send.at[half, pl.ds(0, 7)]
        move(ref, ref, fin_s.at[half], fin_r.at[half], right).wait_send()

    def drain(g, _):
        for way in range(2):
            x_copy(g, way).wait_send()
            x_forward(g, way).wait_send()
        core_copy(g).wait_send()
        return 0

    lax.fori_loop(0, 8, drain, 0)


def per_device(tokens, norm_gain, expert_weights, slot_expert, pair_slots, combine_weights):
    pieces = expert_weights.reshape(NZ * NY, NX, TILES, 128).transpose(0, 2, 1, 3)
    vmem = pl.BlockSpec(memory_space=pltpu.VMEM)
    sem = pltpu.SemaphoreType.DMA
    return pl.pallas_call(
        kernel,
        out_shape=jax.ShapeDtypeStruct((ROWS, D), BF16),
        in_specs=[vmem, vmem, pl.BlockSpec(memory_space=pl.ANY), vmem, vmem, vmem],
        out_specs=vmem,
        scratch_shapes=[
            pltpu.VMEM((8, 8, ROWS, HALF), BF16),
            pltpu.VMEM((8, 8, ROWS, HALF + 128), BF16),
            pltpu.VMEM((2, NX, NZ, NY, TILES, 4, 128), BF16),
            pltpu.VMEM((8, 256, 3 * F), BF16),
            pltpu.VMEM((1024, 2 * F), F32),
            pltpu.VMEM((2, 8, 8, ROWS, F), BF16),
            pltpu.VMEM((2, 8, 128, 128), F32),
            pltpu.VMEM((2, 2, 4, 128, HALF), BF16),
            pltpu.VMEM((2, 2, 4, 128, HALF), BF16),
            pltpu.VMEM((2, 8, ROWS, HALF), BF16),
            pltpu.VMEM((2, 8, ROWS, HALF), BF16),
            sem, sem, sem((2,)), sem((16,)), sem((16,)), sem((8,)), sem, sem,
            sem((2, 8)), sem((2, 8)), sem((2, 8)), sem((2, 8)), sem((8,)), sem((8,)),
            sem((2, 2, 4)), sem((2, 2, 4)), sem((2,)), sem((2,)),
        ],
        compiler_params=pltpu.CompilerParams(
            collective_id=0, has_side_effects=True, vmem_limit_bytes=56 * 2**20),
    )(tokens, norm_gain.reshape(1, D), pieces, slot_expert.astype(F32).reshape(1, 128), pair_slots, combine_weights)


def solution(mesh):
    placed = (
        P(("dp", "rep"), None),
        P(),
        P(None, ("dp", "rep"), None),
        P(),
        P(("dp", "rep"), None),
        P(("dp", "rep"), None),
    )
    return jax.shard_map(
        per_device, mesh=mesh, in_specs=placed, out_specs=P(("dp", "rep"), None), check_vma=False
    )
```

```python
import jax
import jax.numpy as jnp
from jax import lax
from jax.experimental import pallas as pl
from jax.experimental.pallas import tpu as pltpu
from jax.sharding import PartitionSpec as P

NZ, NY, NX = 8, 8, 4
D, F, ROWS = 2048, 768, 16
HALF = D // 2
TILES = 3 * F // 128
BF16, F32 = jnp.bfloat16, jnp.float32


def mod(value, size):
    return lax.rem(value + 2 * size, size)


def kernel(tok_ref, gain_ref, w_ref, slot_ref, pair_ref, comb_ref, out_ref,
           xa, xb, wz, wraw, wmat, acc, hid, coef, terms, rs_send, rs_recv, fin_send, fin_recv,
           sem_a1, sem_b1, sem_s1, ring_r, ring_s, z_recv, z_send, y_recv, y_send, w_own,
           x_recv, x_send, f_recv, f_send, c_recv, c_send,
           rs_r, rs_s, fin_r, fin_s):
    dp, x = lax.axis_index("dp"), lax.axis_index("rep")
    z, y, core = dp // (2 * NY), lax.rem(dp // 2, NY), lax.rem(dp, 2)

    def at(zz, yy):
        return (zz * (2 * NY) + yy * 2 + core, x)

    def move(src, dst, send, recv, device):
        return pltpu.make_async_remote_copy(
            src_ref=src, dst_ref=dst, send_sem=send, recv_sem=recv,
            device_id=device, device_id_type=pl.DeviceIdType.MESH)

    right, left = (dp, mod(x + 1, NX)), (dp, mod(x - 1, NX))
    other = (dp + 1 - 2 * core, x)

    barrier = pltpu.get_barrier_semaphore()

    def greet(i, _):
        for device in (at(mod(z + i, NZ), y), at(z, mod(y + i, NY))):
            pl.semaphore_signal(barrier, inc=1, device_id=device, device_id_type=pl.DeviceIdType.MESH)
        return 0

    lax.fori_loop(1, 8, greet, 0)
    for device in (right, left, other):
        pl.semaphore_signal(barrier, inc=1, device_id=device, device_id_type=pl.DeviceIdType.MESH)

    values = tok_ref[...].astype(F32)
    mean_square = jnp.mean(values * values, axis=1, keepdims=True)
    normed = (values * lax.rsqrt(mean_square + 1e-06) * gain_ref[...]).astype(BF16)
    lane = lax.broadcasted_iota(jnp.int32, (ROWS, 128), 1)
    weights = jnp.zeros((ROWS, 128), F32)
    slots, pairs, combs = slot_ref[...].astype(F32), pair_ref[...].T, comb_ref[...].T
    for k in range(8):
        held = jnp.sum(jnp.where(lane == pairs[:, k:k + 1], slots, 0.0), axis=1, keepdims=True)
        weights = weights + jnp.where((lane & 63).astype(F32) == held, combs[:, k:k + 1], 0.0)
    high = weights.astype(BF16)
    low = (weights - high.astype(F32)).astype(BF16)
    xa[z, y] = normed[:, :HALF]
    xb[y, z, :, :HALF] = normed[:, HALF:]
    xb[y, z, :, HALF:] = jnp.where(lane < 64, high.astype(F32), low.astype(F32)).astype(BF16)

    acc[...] = jnp.zeros_like(acc)
    pl.semaphore_wait(barrier, 17)

    def offset(g):
        half = (g + 1) // 2
        odd = lax.rem(g, 2)
        return odd * half + (1 - odd) * lax.rem(NZ - half, NZ)

    def z_copy(g):
        zz = mod(z + offset(g), NZ)
        return move(w_ref.at[pl.ds(zz * NY, NY)], wz.at[z], z_send.at[g], z_recv.at[g], at(zz, y))

    def y_spread(g, source):
        zz = mod(z - offset(g), NZ)

        def one(i, _):
            yy = mod(y + offset(i), NY)
            move(source(zz, yy), wraw.at[core, x, zz, y], y_send.at[g], y_recv.at[g], at(z, yy)).start()
            return 0

        lax.fori_loop(1, NY, one, 0)
        pltpu.make_async_copy(source(zz, y), wraw.at[core, x, zz, y], w_own.at[g]).start()

    def y_landed(g):
        zz = mod(z - offset(g), NZ)
        ref = wraw.at[core, x, zz, pl.ds(0, 7)]
        move(ref, ref, y_send.at[g], y_recv.at[g], right).wait_recv()
        ref = wraw.at[core, x, zz, y]
        pltpu.make_async_copy(ref, ref, w_own.at[g]).wait()

    z_copy(1).start()
    z_copy(2).start()
    y_spread(0, lambda zz, yy: w_ref.at[zz * NY + yy])

    def first_a(dy):
        return move(xa.at[z, y], xa.at[z, y], sem_s1.at[0], sem_a1, at(z, mod(y + dy, NY)))

    def first_b(dz):
        return move(xb.at[y, z], xb.at[y, z], sem_s1.at[1], sem_b1, at(mod(z + dz, NZ), y))

    def start_first(i, _):
        first_a(offset(i)).start()
        first_b(offset(i)).start()
        return 0

    lax.fori_loop(1, 8, start_first, 0)

    def ring(half, way, step, part, ahead=0):
        sign = 1 - 2 * way
        mine = (z, y)[half]
        device = at(mod(z + sign, NZ), y) if half == 0 else at(z, mod(y + sign, NY))
        ref = (xa, xb)[half].at[mod(mine - sign * (step + ahead), 8), pl.ds(2 * part, 2)]
        index = ((half * 2 + way) * 4 + step) * 4 + part
        return move(ref, ref, ring_s.at[index], ring_r.at[index], device)

    def ring_landed(half, way, step, part):
        ring(half, way, step, part, 1).wait_recv()

    def rows_first():
        move(xa.at[z, pl.ds(0, 7)], xa.at[z, pl.ds(0, 7)], sem_s1.at[0], sem_a1, right).wait_recv()
        move(xb.at[y, pl.ds(0, 7)], xb.at[y, pl.ds(0, 7)], sem_s1.at[1], sem_b1, right).wait_recv()

    def rows_step(j, _):
        step = j // 4
        for half in range(2):
            for way in range(2):
                part = lax.rem(j, 4) + 2 * way * (step // 3)

                @pl.when(step > 0)
                def _(half=half, way=way, part=part):
                    ring_landed(half, way, step - 1, part)

                ring(half, way, step, part).start()
        return 0

    def rows_end():
        for half in range(2):
            for way in range(2):
                for i in range(2):
                    ring_landed(half, way, 2, 2 * (1 - way) + i)
                    ring_landed(half, way, 3, 2 * way + i)
        mine = lax.broadcasted_iota(jnp.int32, (128, 128), 1) & 63
        mine = mine == z * NY + y

        def fill(i, _):
            for half in range(2):
                raw = xb[:, i, :, HALF:] if half == 0 else xb[i, :, :, HALF:]
                c = jnp.where(mine, raw.reshape(128, 128).astype(F32), 0.0)
                coef[half, i] = jnp.broadcast_to(jnp.sum(c, axis=1, keepdims=True), (128, 128))
            return 0

        lax.fori_loop(0, 8, fill, 0)

    def multiply(g, _):
        zz = mod(z - offset(g), NZ)

        def tile(yy, _):
            for c in range(2):
                row = pl.multiple_of(yy * 32 + c * 16, 16)
                for t in range(TILES):
                    wmat[zz, pl.ds(row, 16), t * 128:(t + 1) * 128] = jnp.concatenate(
                        [wraw[c, i, zz, yy, t] for i in range(NX)], axis=0)
            return 0

        lax.fori_loop(0, NY, tile, 0)

        def add(rows_of, first):
            column = pl.multiple_of((zz - first) * 256, 256)

            def part(q, _):
                rows = rows_of(q, column)
                for n in range(3):
                    at_n = slice(n * 512, (n + 1) * 512)
                    spot = pl.ds(pl.multiple_of(q * 512, 512), 512)
                    acc[spot, at_n] += jnp.dot(rows, wmat[zz, :, at_n], preferred_element_type=F32)
                return 0

            lax.fori_loop(0, 2, part, 0)

        @pl.when(zz < 4)
        def _():
            add(lambda q, col: xa[pl.ds(q * 4, 4), :, :, pl.ds(col, 256)].reshape(512, 256), 0)

        @pl.when(zz >= 4)
        def _():
            add(lambda q, col: jnp.concatenate(
                [xb[:, q * 4 + i, :, pl.ds(col, 256)].reshape(128, 256) for i in range(4)], axis=0), 4)

        return 0

    def x_copy(g, way):
        zz = mod(z - offset(g), NZ)
        ref = wraw.at[core, x, zz]
        return move(ref, ref, x_send.at[way, g], x_recv.at[way, g], (right, left)[way])

    def x_forward(g, way):
        zz = mod(z - offset(g), NZ)
        ref = wraw.at[core, mod(x - 1 + 2 * way, NX), zz, pl.ds(4 * way, 4)]
        return move(ref, ref, f_send.at[way, g], f_recv.at[way, g], (right, left)[way])

    def core_copy(g):
        zz = mod(z - offset(g), NZ)
        ref = wraw.at[core, :, zz]
        return move(ref, ref, c_send.at[g], c_recv.at[g], other)

    def w_step(s, _):
        @pl.when(s < 5)
        def _():
            z_copy(s + 3).start()

        @pl.when(s < 7)
        def _():
            z_copy(s + 1).wait_recv()
            y_spread(s + 1, lambda zz, yy: wz.at[zz, yy])

        @pl.when(s < 8)
        def _():
            y_landed(s)
            for way in range(2):
                x_copy(s, way).start()

        pl.when(s == 0)(rows_first)

        @pl.when(s < 5)
        def _():
            lax.fori_loop(3 * s, jnp.minimum(3 * s + 3, 14), rows_step, 0)

        pl.when(s == 5)(rows_end)

        @pl.when((s >= 1) & (s < 9))
        def _():
            for way in range(2):
                x_copy(s - 1, way).wait_recv()
                x_forward(s - 1, way).start()

        @pl.when((s >= 2) & (s < 10))
        def _():
            for way in range(2):
                x_forward(s - 2, way).wait_recv()
            core_copy(s - 2).start()

        @pl.when((s >= 3) & (s < 11))
        def _():
            core_copy(s - 3).wait_recv()

        @pl.when(s == 5)
        def _():
            lax.fori_loop(0, 3, multiply, 0)

        @pl.when(s > 5)
        def _():
            multiply(s - 3, 0)

        return 0

    lax.fori_loop(0, 11, w_step, 0)

    def activate(i, _):
        spot = pl.ds(pl.multiple_of(i * 128, 128), 128)
        gate, up = acc[spot, :F], acc[spot, F:]
        value = (gate / (1.0 + jnp.exp(-gate)) * up).astype(BF16).reshape(8, ROWS, F)
        hid[0, i] = value
        hid[1, :, i] = value
        return 0

    lax.fori_loop(0, 8, activate, 0)

    def term(half, index):
        rows = hid[half, index].reshape(128, F)
        scale = coef[half, index][:, :1]
        parts = [lax.dot_general(rows, wmat[half * 4 + i, :, 2 * F:], (((1,), (1,)), ((), ())),
                                 preferred_element_type=F32) for i in range(4)]
        return jnp.concatenate(parts, axis=1) * scale

    def beside(half, sign):
        return at(mod(z + (1 - half) * sign, NZ), mod(y + half * sign, NY))

    def mine_of(half):
        return (1 - half) * z + half * y

    def rs_rows(way, part):
        start = 64 * way if part else 64 - 64 * way
        return slice(start, start + 64)

    def rs_copy(half, way, step, part):
        rows = pl.ds(rs_rows(way, part).start, 64)
        return move(rs_send.at[half, way, step, rows], rs_recv.at[half, way, step, rows],
                    rs_s.at[half, way, step, part], rs_r.at[half, way, step, part], beside(half, 1 - 2 * way))

    def begin(half, _):
        value = term(half, mod(mine_of(half) + 4, 8)).astype(BF16)
        for way in range(2):
            rs_send[half, way, 0, rs_rows(way, 1)] = value[rs_rows(way, 1)]
            rs_copy(half, way, 0, 1).start()
        return 0

    lax.fori_loop(0, 2, begin, 0)

    def go(step, _):
        def prepare(half, _):
            for way in range(2):
                terms[half, way] = term(half, mod(mine_of(half) + (1 - 2 * way) * (4 - step), 8))
            return 0

        lax.fori_loop(0, 2, prepare, 0)

        def pass_on(half, part, way, first):
            rows = rs_rows(way, part)
            value = terms[half, way, rows]
            if not first:
                rs_copy(half, way, step - 1, part).wait_recv()
                value = value + rs_recv[half, way, step - 1, rows].astype(F32)
            rs_send[half, way, step, rows] = value.astype(BF16)
            rs_copy(half, way, step, part).start()

        for part in range(2):
            def each(half, _):
                for way in range(2):
                    if part == 0:
                        pl.when(step == 1)(lambda: pass_on(half, part, way, True))
                        pl.when(step > 1)(lambda: pass_on(half, part, way, False))
                    else:
                        pass_on(half, part, way, False)
                return 0

            lax.fori_loop(0, 2, each, 0)
        return 0

    def fin_spread(half, there):
        mine = (1 - half) * y + half * z
        device = at((1 - half) * z + half * there, (1 - half) * there + half * y)

        @pl.when(there != mine)
        def _():
            move(fin_send.at[half, there], fin_recv.at[half, mine], fin_s.at[half], fin_r.at[half], device).start()

    def end(half, _):
        terms[half, 0] = term(half, mine_of(half))
        for part in range(2):
            rows = slice(64 * part, 64 * part + 64)
            value = terms[half, 0, rows]
            for way in range(2):
                rs_copy(half, way, 3, int(part == way)).wait_recv()
                value = value + rs_recv[half, way, 3, rows].astype(F32)
            fin_send[half, 4 * part:4 * part + 4] = value.astype(BF16).reshape(4, ROWS, HALF)
            for i in range(4):
                fin_spread(half, 4 * part + i)
        mine = (1 - half) * y + half * z
        fin_recv[half, mine] = fin_send[half, mine]
        return 0

    lax.fori_loop(1, 4, go, 0)
    lax.fori_loop(0, 2, end, 0)

    for half in range(2):
        ref = fin_recv.at[half, pl.ds(0, 7)]
        move(ref, ref, fin_s.at[half], fin_r.at[half], right).wait_recv()
        total = fin_recv[half, 0].astype(F32)
        for i in range(1, 8):
            total = total + fin_recv[half, i].astype(F32)
        out_ref[:, half * HALF:(half + 1) * HALF] = total.astype(BF16)

    move(xa.at[z, pl.ds(0, 7)], xa.at[z, pl.ds(0, 7)], sem_s1.at[0], sem_a1, right).wait_send()
    move(xb.at[y, pl.ds(0, 7)], xb.at[y, pl.ds(0, 7)], sem_s1.at[1], sem_b1, right).wait_send()
    for half in range(2):
        for way in range(2):
            rs_copy(half, way, 0, 1).wait_send()
            for step in range(1, 4):
                for part in range(2):
                    rs_copy(half, way, step, part).wait_send()
        ref = fin_send.at[half, pl.ds(0, 7)]
        move(ref, ref, fin_s.at[half], fin_r.at[half], right).wait_send()

    def ring_drain(j, _):
        step = j // 4
        for half in range(2):
            for way in range(2):
                ring(half, way, step, lax.rem(j, 4) + 2 * way * (step // 3)).wait_send()
        return 0

    lax.fori_loop(0, 14, ring_drain, 0)

    def drain(g, _):
        for way in range(2):
            x_copy(g, way).wait_send()
            x_forward(g, way).wait_send()
        core_copy(g).wait_send()
        ref = wz.at[0, pl.ds(0, 7)]
        move(ref, ref, y_send.at[g], y_recv.at[g], right).wait_send()

        @pl.when(g > 0)
        def _():
            z_copy(g).wait_send()

        return 0

    lax.fori_loop(0, 8, drain, 0)


def per_device(tokens, norm_gain, expert_weights, slot_expert, pair_slots, combine_weights):
    pieces = expert_weights.reshape(NZ * NY, NX, TILES, 128).transpose(0, 2, 1, 3)
    vmem = pl.BlockSpec(memory_space=pltpu.VMEM)
    sem = pltpu.SemaphoreType.DMA
    return pl.pallas_call(
        kernel,
        out_shape=jax.ShapeDtypeStruct((ROWS, D), BF16),
        in_specs=[vmem, vmem, pl.BlockSpec(memory_space=pl.ANY), vmem, vmem, vmem],
        out_specs=vmem,
        scratch_shapes=[
            pltpu.VMEM((8, 8, ROWS, HALF), BF16),
            pltpu.VMEM((8, 8, ROWS, HALF + 128), BF16),
            pltpu.VMEM((NZ, NY, TILES, 4, 128), BF16),
            pltpu.VMEM((2, NX, NZ, NY, TILES, 4, 128), BF16),
            pltpu.VMEM((8, 256, 3 * F), BF16),
            pltpu.VMEM((1024, 2 * F), F32),
            pltpu.VMEM((2, 8, 8, ROWS, F), BF16),
            pltpu.VMEM((2, 8, 128, 128), F32),
            pltpu.VMEM((2, 2, 128, HALF), F32),
            pltpu.VMEM((2, 2, 4, 128, HALF), BF16),
            pltpu.VMEM((2, 2, 4, 128, HALF), BF16),
            pltpu.VMEM((2, 8, ROWS, HALF), BF16),
            pltpu.VMEM((2, 8, ROWS, HALF), BF16),
            sem, sem, sem((2,)), sem((64,)), sem((64,)), sem((8,)), sem((8,)), sem((8,)), sem((8,)), sem((8,)),
            sem((2, 8)), sem((2, 8)), sem((2, 8)), sem((2, 8)), sem((8,)), sem((8,)),
            sem((2, 2, 4, 2)), sem((2, 2, 4, 2)), sem((2,)), sem((2,)),
        ],
        compiler_params=pltpu.CompilerParams(
            collective_id=0, has_side_effects=True, vmem_limit_bytes=56 * 2**20),
    )(tokens, norm_gain.reshape(1, D), pieces, slot_expert.reshape(1, 128), pair_slots.T, combine_weights.T)


def solution(mesh):
    placed = (
        P(("dp", "rep"), None),
        P(),
        P(None, ("dp", "rep"), None),
        P(),
        P(("dp", "rep"), None),
        P(("dp", "rep"), None),
    )
    return jax.shard_map(
        per_device, mesh=mesh, in_specs=placed, out_specs=P(("dp", "rep"), None), check_vma=False
    )
```

```python
import jax
import jax.numpy as jnp
from jax import lax
from jax.experimental import pallas as pl
from jax.experimental.pallas import tpu as pltpu
from jax.sharding import PartitionSpec as P

NZ, NY, NX = 8, 8, 4
D, F, ROWS = 2048, 768, 16
HALF = D // 2
TILES = 3 * F // 128
BF16, F32 = jnp.bfloat16, jnp.float32
FIRST, RING, READY, SLOTS = 0, 4, 9, 3


def mod(value, size):
    return lax.rem(value + 2 * size, size)


def kernel(tok_ref, gain_ref, w_ref, slot_ref, pair_ref, comb_ref, out_ref,
           xa, xb, wz, wraw, wmat, acc, hid, coef, terms, rs_send, rs_recv, fin_send, fin_recv,
           first_r, first_s, ring_r, ring_s, z_recv, z_send, y_recv, y_send, w_own,
           x_recv, x_send, f_recv, f_send, c_recv, c_send,
           rs_r, rs_s, fin_r, fin_s):
    dp, x = lax.axis_index("dp"), lax.axis_index("rep")
    z, y, core = dp // (2 * NY), lax.rem(dp // 2, NY), lax.rem(dp, 2)

    def at(zz, yy):
        return (zz * (2 * NY) + yy * 2 + core, x)

    def move(src, dst, send, recv, device):
        return pltpu.make_async_remote_copy(
            src_ref=src, dst_ref=dst, send_sem=send, recv_sem=recv,
            device_id=device, device_id_type=pl.DeviceIdType.MESH)

    right, left = (dp, mod(x + 1, NX)), (dp, mod(x - 1, NX))
    other = (dp + 1 - 2 * core, x)

    barrier = pltpu.get_barrier_semaphore()

    def greet(i, _):
        for device in (at(mod(z + i, NZ), y), at(z, mod(y + i, NY))):
            pl.semaphore_signal(barrier, inc=1, device_id=device, device_id_type=pl.DeviceIdType.MESH)
        return 0

    lax.fori_loop(1, 8, greet, 0)
    for device in (right, left, other):
        pl.semaphore_signal(barrier, inc=1, device_id=device, device_id_type=pl.DeviceIdType.MESH)

    acc[...] = jnp.zeros_like(acc)
    pl.semaphore_wait(barrier, 17)

    def offset(g):
        half = (g + 1) // 2
        odd = lax.rem(g, 2)
        return odd * half + (1 - odd) * lax.rem(NZ - half, NZ)

    def z_copy(g):
        zz = mod(z + offset(g), NZ)
        return move(w_ref.at[pl.ds(zz * NY, NY)], wz.at[z], z_send.at[g], z_recv.at[g], at(zz, y))

    def y_spread(g, source):
        zz = mod(z - offset(g), NZ)

        def one(i, _):
            yy = mod(y + offset(i), NY)
            move(source(zz, yy), wraw.at[core, x, zz, y], y_send.at[g], y_recv.at[g], at(z, yy)).start()
            return 0

        lax.fori_loop(1, NY, one, 0)
        pltpu.make_async_copy(source(zz, y), wraw.at[core, x, zz, y], w_own.at[g]).start()

    def y_landed(g):
        zz = mod(z - offset(g), NZ)
        ref = wraw.at[core, x, zz, pl.ds(0, 7)]
        move(ref, ref, y_send.at[g], y_recv.at[g], right).wait_recv()
        ref = wraw.at[core, x, zz, y]
        pltpu.make_async_copy(ref, ref, w_own.at[g]).wait()

    y_spread(0, lambda zz, yy: w_ref.at[zz * NY + yy])
    for g in range(1, 5):
        z_copy(g).start()

    values = tok_ref[...].astype(F32)
    mean_square = jnp.mean(values * values, axis=1, keepdims=True)
    normed = (values * lax.rsqrt(mean_square + 1e-06) * gain_ref[...]).astype(BF16)
    lane = lax.broadcasted_iota(jnp.int32, (ROWS, 128), 1)
    weights = jnp.zeros((ROWS, 128), F32)
    slots, pairs, combs = slot_ref[...].astype(F32), pair_ref[...].T, comb_ref[...].T
    for k in range(8):
        held = jnp.sum(jnp.where(lane == pairs[:, k:k + 1], slots, 0.0), axis=1, keepdims=True)
        weights = weights + jnp.where((lane & 63).astype(F32) == held, combs[:, k:k + 1], 0.0)
    high = weights.astype(BF16)
    low = (weights - high.astype(F32)).astype(BF16)
    xa[z, y] = normed[:, :HALF]
    xb[y, z, :, :HALF] = normed[:, HALF:]
    xb[y, z, :, HALF:] = jnp.where(lane < 64, high.astype(F32), low.astype(F32)).astype(BF16)

    def first(half, way, step, ahead=0):
        sign = 1 - 2 * way
        mine = (y, z)[half]
        device = at(z, mod(y + sign, NY)) if half == 0 else at(mod(z + sign, NZ), y)
        ref = (xa.at[z], xb.at[y])[half].at[mod(mine - sign * (step + ahead), 8)]
        index = (half * 2 + way) * 4 + step
        return move(ref, ref, first_s.at[index], first_r.at[index], device)

    def first_step(step):
        for half in range(2):
            for way in range(2):
                if step > 0 and (way == half or step < 4):
                    first(half, way, step - 1, 1).wait_recv()
                if step < 3 + (way == half):
                    first(half, way, step).start()

    def ring(half, way, step, part, ahead=0):
        sign = 1 - 2 * way
        mine = (z, y)[half]
        device = at(mod(z + sign, NZ), y) if half == 0 else at(z, mod(y + sign, NY))
        ref = (xa, xb)[half].at[mod(mine - sign * (step + ahead), 8), pl.ds(2 * part, 2)]
        index = ((half * 2 + way) * 4 + step) * 4 + part
        return move(ref, ref, ring_s.at[index], ring_r.at[index], device)

    def ring_landed(half, way, step, part):
        ring(half, way, step, part, 1).wait_recv()

    def rows_step(j, _):
        step = j // 4
        for half in range(2):
            for way in range(2):
                part = lax.rem(j, 4) + 2 * way * (step // 3)

                @pl.when(step > 0)
                def _(half=half, way=way, part=part):
                    ring_landed(half, way, step - 1, part)

                ring(half, way, step, part).start()
        return 0

    def rows_end():
        for half in range(2):
            for way in range(2):
                for i in range(2):
                    ring_landed(half, way, 2, 2 * (1 - way) + i)
                    ring_landed(half, way, 3, 2 * way + i)
        mine = lax.broadcasted_iota(jnp.int32, (128, 128), 1) & 63
        mine = mine == z * NY + y

        def fill(i, _):
            for half in range(2):
                raw = xb[:, i, :, HALF:] if half == 0 else xb[i, :, :, HALF:]
                c = jnp.where(mine, raw.reshape(128, 128).astype(F32), 0.0)
                coef[half, i] = jnp.broadcast_to(jnp.sum(c, axis=1, keepdims=True), (128, 128))
            return 0

        lax.fori_loop(0, 8, fill, 0)

    def place(g):
        zz = mod(z - offset(g), NZ)

        def tile(yy, _):
            for c in range(2):
                row = pl.multiple_of(yy * 32 + c * 16, 16)
                for t in range(TILES):
                    wmat[zz, pl.ds(row, 16), t * 128:(t + 1) * 128] = jnp.concatenate(
                        [wraw[c, i, zz, yy, t] for i in range(NX)], axis=0)
            return 0

        lax.fori_loop(0, NY, tile, 0)

    def multiply(g, _):
        zz = mod(z - offset(g), NZ)

        def add(rows_of, first):
            column = pl.multiple_of((zz - first) * 256, 256)

            def part(q, _):
                rows = rows_of(q, column)
                for n in range(3):
                    at_n = slice(n * 512, (n + 1) * 512)
                    part_of = jnp.dot(rows, wmat[zz, :, at_n], preferred_element_type=F32)
                    acc[pl.ds(q * 4, 4), :, :, at_n] += part_of.reshape(4, 8, ROWS, 512)
                return 0

            lax.fori_loop(0, 2, part, 0)

        @pl.when(zz < 4)
        def _():
            add(lambda q, col: xa[pl.ds(q * 4, 4), :, :, pl.ds(col, 256)].reshape(512, 256), 0)

        @pl.when(zz >= 4)
        def _():
            add(lambda q, col: jnp.concatenate(
                [xb[:, q * 4 + i, :, pl.ds(col, 256)].reshape(128, 256) for i in range(4)], axis=0), 4)

        return 0

    def x_copy(g, way):
        zz = mod(z - offset(g), NZ)
        ref = wraw.at[core, x, zz]
        return move(ref, ref, x_send.at[way, g], x_recv.at[way, g], (right, left)[way])

    def x_forward(g, way):
        zz = mod(z - offset(g), NZ)
        ref = wraw.at[core, mod(x - 1 + 2 * way, NX), zz, pl.ds(4 * way, 4)]
        return move(ref, ref, f_send.at[way, g], f_recv.at[way, g], (right, left)[way])

    def core_copy(g):
        zz = mod(z - offset(g), NZ)
        ref = wraw.at[core, :, zz]
        return move(ref, ref, c_send.at[g], c_recv.at[g], other)

    def w_step(s, _):
        @pl.when(s < 3)
        def _():
            z_copy(s + 5).start()

        @pl.when(s < 6)
        def _():
            z_copy(s + 2).wait_recv()
            y_spread(s + 2, lambda zz, yy: wz.at[zz, yy])

        @pl.when(s < 8)
        def _():
            y_landed(s)
            for way in range(2):
                x_copy(s, way).start()

        for i in range(5):
            pl.when(s == FIRST + i)(lambda i=i: first_step(i))

        @pl.when((s >= RING) & (s < READY))
        def _():
            lax.fori_loop(SLOTS * (s - RING), jnp.minimum(SLOTS * (s - RING + 1), 14), rows_step, 0)

        pl.when(s == READY)(rows_end)

        @pl.when((s >= 2) & (s < 10))
        def _():
            for way in range(2):
                x_copy(s - 2, way).wait_recv()
                x_forward(s - 2, way).start()

        @pl.when((s >= 4) & (s < 12))
        def _():
            for way in range(2):
                x_forward(s - 4, way).wait_recv()
            core_copy(s - 4).start()

        @pl.when(s >= 5)
        def _():
            core_copy(s - 5).wait_recv()
            place(s - 5)

        @pl.when(s == READY)
        def _():
            lax.fori_loop(0, READY - 4, multiply, 0)

        @pl.when(s > READY)
        def _():
            multiply(s - 5, 0)

        return 0

    z_copy(1).wait_recv()
    y_spread(1, lambda zz, yy: wz.at[zz, yy])
    lax.fori_loop(0, 13, w_step, 0)

    def activate(rows):
        gate, up = rows[:, :F], rows[:, F:]
        hid[...] = (gate / (1.0 + jnp.exp(-gate)) * up).astype(BF16)

    def term(half, index):
        pl.when(half == 0)(lambda: activate(acc[index].reshape(128, 2 * F)))
        pl.when(half == 1)(lambda: activate(acc[:, index].reshape(128, 2 * F)))
        rows = hid[...]
        scale = coef[half, index][:, :1]
        parts = [lax.dot_general(rows, wmat[half * 4 + i, :, 2 * F:], (((1,), (1,)), ((), ())),
                                 preferred_element_type=F32) for i in range(4)]
        return jnp.concatenate(parts, axis=1) * scale

    def beside(half, sign):
        return at(mod(z + (1 - half) * sign, NZ), mod(y + half * sign, NY))

    def mine_of(half):
        return (1 - half) * z + half * y

    def rs_rows(way, part):
        start = 64 * way if part else 64 - 64 * way
        return slice(start, start + 64)

    def rs_copy(half, way, step, part):
        rows = pl.ds(rs_rows(way, part).start, 64)
        return move(rs_send.at[half, way, step, rows], rs_recv.at[half, way, step, rows],
                    rs_s.at[half, way, step, part], rs_r.at[half, way, step, part], beside(half, 1 - 2 * way))

    def begin(half, _):
        value = term(half, mod(mine_of(half) + 4, 8)).astype(BF16)
        for way in range(2):
            rs_send[half, way, 0, rs_rows(way, 1)] = value[rs_rows(way, 1)]
            rs_copy(half, way, 0, 1).start()
        return 0

    lax.fori_loop(0, 2, begin, 0)

    def go(step, _):
        def prepare(half, way):
            terms[half, way] = term(half, mod(mine_of(half) + (1 - 2 * way) * (4 - step), 8))

        def pass_on(half, part, way, first):
            rows = rs_rows(way, part)
            value = terms[half, way, rows]
            if not first:
                rs_copy(half, way, step - 1, part).wait_recv()
                value = value + rs_recv[half, way, step - 1, rows].astype(F32)
            rs_send[half, way, step, rows] = value.astype(BF16)
            rs_copy(half, way, step, part).start()

        for part in range(2):
            def each(half, _):
                for way in range(2):
                    if part == 0:
                        prepare(half, way)
                        pl.when(step == 1)(lambda: pass_on(half, part, way, True))
                        pl.when(step > 1)(lambda: pass_on(half, part, way, False))
                    else:
                        pass_on(half, part, way, False)
                return 0

            lax.fori_loop(0, 2, each, 0)
        return 0

    def fin_spread(half, there):
        mine = (1 - half) * y + half * z
        device = at((1 - half) * z + half * there, (1 - half) * there + half * y)

        @pl.when(there != mine)
        def _():
            move(fin_send.at[half, there], fin_recv.at[half, mine], fin_s.at[half], fin_r.at[half], device).start()

    def end(half, _):
        terms[half, 0] = term(half, mine_of(half))
        for part in range(2):
            rows = slice(64 * part, 64 * part + 64)
            value = terms[half, 0, rows]
            for way in range(2):
                rs_copy(half, way, 3, int(part == way)).wait_recv()
                value = value + rs_recv[half, way, 3, rows].astype(F32)
            fin_send[half, 4 * part:4 * part + 4] = value.astype(BF16).reshape(4, ROWS, HALF)
            for i in range(4):
                fin_spread(half, 4 * part + i)
        mine = (1 - half) * y + half * z
        fin_recv[half, mine] = fin_send[half, mine]
        return 0

    lax.fori_loop(1, 4, go, 0)
    lax.fori_loop(0, 2, end, 0)

    for half in range(2):
        for way in range(2):
            for step in range(3 + (way == half)):
                first(half, way, step).wait_send()
    for half in range(2):
        for way in range(2):
            rs_copy(half, way, 0, 1).wait_send()
            for step in range(1, 4):
                for part in range(2):
                    rs_copy(half, way, step, part).wait_send()

    def ring_drain(j, _):
        step = j // 4
        for half in range(2):
            for way in range(2):
                ring(half, way, step, lax.rem(j, 4) + 2 * way * (step // 3)).wait_send()
        return 0

    lax.fori_loop(0, 14, ring_drain, 0)

    def drain(g, _):
        for way in range(2):
            x_copy(g, way).wait_send()
            x_forward(g, way).wait_send()
        core_copy(g).wait_send()
        ref = wz.at[0, pl.ds(0, 7)]
        move(ref, ref, y_send.at[g], y_recv.at[g], right).wait_send()

        @pl.when(g > 0)
        def _():
            z_copy(g).wait_send()

        return 0

    lax.fori_loop(0, 8, drain, 0)

    for half in range(2):
        ref = fin_recv.at[half, pl.ds(0, 7)]
        move(ref, ref, fin_s.at[half], fin_r.at[half], right).wait_recv()
        total = fin_recv[half, 0].astype(F32)
        for i in range(1, 8):
            total = total + fin_recv[half, i].astype(F32)
        out_ref[:, half * HALF:(half + 1) * HALF] = total.astype(BF16)
        ref = fin_send.at[half, pl.ds(0, 7)]
        move(ref, ref, fin_s.at[half], fin_r.at[half], right).wait_send()


def per_device(tokens, norm_gain, expert_weights, slot_expert, pair_slots, combine_weights):
    pieces = expert_weights.reshape(NZ * NY, NX, TILES, 128).transpose(0, 2, 1, 3)
    vmem = pl.BlockSpec(memory_space=pltpu.VMEM)
    sem = pltpu.SemaphoreType.DMA
    return pl.pallas_call(
        kernel,
        out_shape=jax.ShapeDtypeStruct((ROWS, D), BF16),
        in_specs=[vmem, vmem, pl.BlockSpec(memory_space=pl.ANY), vmem, vmem, vmem],
        out_specs=vmem,
        scratch_shapes=[
            pltpu.VMEM((8, 8, ROWS, HALF), BF16),
            pltpu.VMEM((8, 8, ROWS, HALF + 128), BF16),
            pltpu.VMEM((NZ, NY, TILES, 4, 128), BF16),
            pltpu.VMEM((2, NX, NZ, NY, TILES, 4, 128), BF16),
            pltpu.VMEM((8, 256, 3 * F), BF16),
            pltpu.VMEM((8, 8, ROWS, 2 * F), F32),
            pltpu.VMEM((128, F), BF16),
            pltpu.VMEM((2, 8, 128, 128), F32),
            pltpu.VMEM((2, 2, 128, HALF), F32),
            pltpu.VMEM((2, 2, 4, 128, HALF), BF16),
            pltpu.VMEM((2, 2, 4, 128, HALF), BF16),
            pltpu.VMEM((2, 8, ROWS, HALF), BF16),
            pltpu.VMEM((2, 8, ROWS, HALF), BF16),
            sem((16,)), sem((16,)), sem((64,)), sem((64,)), sem((8,)), sem((8,)), sem((8,)), sem((8,)), sem((8,)),
            sem((2, 8)), sem((2, 8)), sem((2, 8)), sem((2, 8)), sem((8,)), sem((8,)),
            sem((2, 2, 4, 2)), sem((2, 2, 4, 2)), sem((2,)), sem((2,)),
        ],
        compiler_params=pltpu.CompilerParams(
            collective_id=0, has_side_effects=True, vmem_limit_bytes=56 * 2**20),
    )(tokens, norm_gain.reshape(1, D), pieces, slot_expert.reshape(1, 128), pair_slots.T, combine_weights.T)


def solution(mesh):
    placed = (
        P(("dp", "rep"), None),
        P(),
        P(None, ("dp", "rep"), None),
        P(),
        P(("dp", "rep"), None),
        P(("dp", "rep"), None),
    )
    return jax.shard_map(
        per_device, mesh=mesh, in_specs=placed, out_specs=P(("dp", "rep"), None), check_vma=False
    )
```

```python
import jax
import jax.numpy as jnp
from jax import lax
from jax.experimental import pallas as pl
from jax.experimental.pallas import tpu as pltpu
from jax.sharding import PartitionSpec as P

NZ, NY, NX = 8, 8, 4
D, F, ROWS = 2048, 768, 16
HALF = D // 2
TILES = 3 * F // 128
BF16, F32 = jnp.bfloat16, jnp.float32
FIRST, RING, READY, SLOTS = 0, 4, 11, 2


def mod(value, size):
    return lax.rem(value + 2 * size, size)


def kernel(tok_ref, gain_ref, w_ref, slot_ref, pair_ref, comb_ref, out_ref,
           xa, xb, wz, wraw, wmat, acc, hid, coef, terms, rs_send, rs_recv, fin_send, fin_recv,
           first_r, first_s, ring_r, ring_s, z_recv, z_send, y_recv, y_send, w_own,
           x_recv, x_send, f_recv, f_send, c_recv, c_send,
           rs_r, rs_s, fin_r, fin_s):
    dp, x = lax.axis_index("dp"), lax.axis_index("rep")
    z, y, core = dp // (2 * NY), lax.rem(dp // 2, NY), lax.rem(dp, 2)

    def at(zz, yy):
        return (zz * (2 * NY) + yy * 2 + core, x)

    def move(src, dst, send, recv, device):
        return pltpu.make_async_remote_copy(
            src_ref=src, dst_ref=dst, send_sem=send, recv_sem=recv,
            device_id=device, device_id_type=pl.DeviceIdType.MESH)

    right, left = (dp, mod(x + 1, NX)), (dp, mod(x - 1, NX))
    other = (dp + 1 - 2 * core, x)

    barrier = pltpu.get_barrier_semaphore()

    def greet(i, _):
        for device in (at(mod(z + i, NZ), y), at(z, mod(y + i, NY))):
            pl.semaphore_signal(barrier, inc=1, device_id=device, device_id_type=pl.DeviceIdType.MESH)
        return 0

    lax.fori_loop(1, 8, greet, 0)
    for device in (right, left, other):
        pl.semaphore_signal(barrier, inc=1, device_id=device, device_id_type=pl.DeviceIdType.MESH)

    acc[...] = jnp.zeros_like(acc)
    pl.semaphore_wait(barrier, 17)

    def offset(g):
        half = (g + 1) // 2
        odd = lax.rem(g, 2)
        return odd * half + (1 - odd) * lax.rem(NZ - half, NZ)

    def z_copy(g):
        zz = mod(z + offset(g), NZ)
        return move(w_ref.at[pl.ds(zz * NY, NY)], wz.at[z], z_send.at[g], z_recv.at[g], at(zz, y))

    def y_spread(g, source):
        zz = mod(z - offset(g), NZ)

        def one(i, _):
            yy = mod(y + offset(i), NY)
            move(source(zz, yy), wraw.at[core, x, zz, y], y_send.at[g], y_recv.at[g], at(z, yy)).start()
            return 0

        lax.fori_loop(1, NY, one, 0)
        pltpu.make_async_copy(source(zz, y), wraw.at[core, x, zz, y], w_own.at[g]).start()

    def y_landed(g):
        zz = mod(z - offset(g), NZ)
        ref = wraw.at[core, x, zz, pl.ds(0, 7)]
        move(ref, ref, y_send.at[g], y_recv.at[g], right).wait_recv()
        ref = wraw.at[core, x, zz, y]
        pltpu.make_async_copy(ref, ref, w_own.at[g]).wait()

    y_spread(0, lambda zz, yy: w_ref.at[zz * NY + yy])
    for g in range(1, 5):
        z_copy(g).start()

    values = tok_ref[...].astype(F32)
    mean_square = jnp.mean(values * values, axis=1, keepdims=True)
    normed = (values * lax.rsqrt(mean_square + 1e-06) * gain_ref[...]).astype(BF16)
    lane = lax.broadcasted_iota(jnp.int32, (ROWS, 128), 1)
    weights = jnp.zeros((ROWS, 128), F32)
    slots, pairs, combs = slot_ref[...].astype(F32), pair_ref[...].T, comb_ref[...].T
    for k in range(8):
        held = jnp.sum(jnp.where(lane == pairs[:, k:k + 1], slots, 0.0), axis=1, keepdims=True)
        weights = weights + jnp.where((lane & 63).astype(F32) == held, combs[:, k:k + 1], 0.0)
    high = weights.astype(BF16)
    low = (weights - high.astype(F32)).astype(BF16)
    xa[z, y] = normed[:, :HALF]
    xb[y, z, :, :HALF] = normed[:, HALF:]
    xb[y, z, :, HALF:] = jnp.where(lane < 64, high.astype(F32), low.astype(F32)).astype(BF16)

    def first(half, way, step, ahead=0):
        sign = 1 - 2 * way
        mine = (y, z)[half]
        device = at(z, mod(y + sign, NY)) if half == 0 else at(mod(z + sign, NZ), y)
        ref = (xa.at[z], xb.at[y])[half].at[mod(mine - sign * (step + ahead), 8)]
        index = (half * 2 + way) * 4 + step
        return move(ref, ref, first_s.at[index], first_r.at[index], device)

    def first_step(step):
        for half in range(2):
            for way in range(2):
                if step > 0 and (way == half or step < 4):
                    first(half, way, step - 1, 1).wait_recv()
                if step < 3 + (way == half):
                    first(half, way, step).start()

    def ring(half, way, step, part, ahead=0):
        sign = 1 - 2 * way
        mine = (z, y)[half]
        device = at(mod(z + sign, NZ), y) if half == 0 else at(z, mod(y + sign, NY))
        ref = (xa, xb)[half].at[mod(mine - sign * (step + ahead), 8), pl.ds(2 * part, 2)]
        index = ((half * 2 + way) * 4 + step) * 4 + part
        return move(ref, ref, ring_s.at[index], ring_r.at[index], device)

    def ring_landed(half, way, step, part):
        ring(half, way, step, part, 1).wait_recv()

    def rows_step(j, _):
        step = j // 4
        for half in range(2):
            for way in range(2):
                part = lax.rem(j, 4) + 2 * way * (step // 3)

                @pl.when(step > 0)
                def _(half=half, way=way, part=part):
                    ring_landed(half, way, step - 1, part)

                ring(half, way, step, part).start()
        return 0

    def rows_end():
        for half in range(2):
            for way in range(2):
                for i in range(2):
                    ring_landed(half, way, 2, 2 * (1 - way) + i)
                    ring_landed(half, way, 3, 2 * way + i)
        mine = lax.broadcasted_iota(jnp.int32, (128, 128), 1) & 63
        mine = mine == z * NY + y

        def fill(i, _):
            for half in range(2):
                raw = xb[:, i, :, HALF:] if half == 0 else xb[i, :, :, HALF:]
                c = jnp.where(mine, raw.reshape(128, 128).astype(F32), 0.0)
                coef[half, i] = jnp.broadcast_to(jnp.sum(c, axis=1, keepdims=True), (128, 128))
            return 0

        lax.fori_loop(0, 8, fill, 0)

    def place(g):
        zz = mod(z - offset(g), NZ)

        def tile(yy, _):
            for c in range(2):
                row = pl.multiple_of(yy * 32 + c * 16, 16)
                for t in range(TILES):
                    wmat[zz, pl.ds(row, 16), t * 128:(t + 1) * 128] = jnp.concatenate(
                        [wraw[c, i, zz, yy, t] for i in range(NX)], axis=0)
            return 0

        lax.fori_loop(0, NY, tile, 0)

    def multiply(g, _):
        zz = mod(z - offset(g), NZ)

        def add(rows_of, first):
            column = pl.multiple_of((zz - first) * 256, 256)

            rows = rows_of(column)
            for n in range(3):
                at_n = slice(n * 512, (n + 1) * 512)
                part_of = jnp.dot(rows, wmat[zz, :, at_n], preferred_element_type=F32)
                acc[:, :, :, at_n] += part_of.reshape(8, 8, ROWS, 512)

        @pl.when(zz < 4)
        def _():
            add(lambda col: xa[:, :, :, pl.ds(col, 256)].reshape(1024, 256), 0)

        @pl.when(zz >= 4)
        def _():
            add(lambda col: jnp.concatenate(
                [xb[:, i, :, pl.ds(col, 256)].reshape(128, 256) for i in range(8)], axis=0), 4)

        return 0

    def x_copy(g, way):
        zz = mod(z - offset(g), NZ)
        ref = wraw.at[core, x, zz]
        return move(ref, ref, x_send.at[way, g], x_recv.at[way, g], (right, left)[way])

    def x_forward(g, way):
        zz = mod(z - offset(g), NZ)
        ref = wraw.at[core, mod(x - 1 + 2 * way, NX), zz, pl.ds(4 * way, 4)]
        return move(ref, ref, f_send.at[way, g], f_recv.at[way, g], (right, left)[way])

    def core_copy(g):
        zz = mod(z - offset(g), NZ)
        ref = wraw.at[core, :, zz]
        return move(ref, ref, c_send.at[g], c_recv.at[g], other)

    def w_step(s, _):
        @pl.when(s < 3)
        def _():
            z_copy(s + 5).start()

        @pl.when(s < 6)
        def _():
            z_copy(s + 2).wait_recv()
            y_spread(s + 2, lambda zz, yy: wz.at[zz, yy])

        @pl.when(s < 8)
        def _():
            y_landed(s)
            for way in range(2):
                x_copy(s, way).start()

        for i in range(5):
            pl.when(s == FIRST + i)(lambda i=i: first_step(i))

        @pl.when((s >= RING) & (s < READY))
        def _():
            lax.fori_loop(SLOTS * (s - RING), jnp.minimum(SLOTS * (s - RING + 1), 14), rows_step, 0)

        pl.when(s == READY)(rows_end)

        @pl.when((s >= 2) & (s < 10))
        def _():
            for way in range(2):
                x_copy(s - 2, way).wait_recv()
                x_forward(s - 2, way).start()

        @pl.when((s >= 4) & (s < 12))
        def _():
            for way in range(2):
                x_forward(s - 4, way).wait_recv()
            core_copy(s - 4).start()

        @pl.when(s >= 5)
        def _():
            core_copy(s - 5).wait_recv()
            place(s - 5)

        @pl.when(s == READY)
        def _():
            lax.fori_loop(0, READY - 4, multiply, 0)

        @pl.when(s > READY)
        def _():
            multiply(s - 5, 0)

        return 0

    z_copy(1).wait_recv()
    y_spread(1, lambda zz, yy: wz.at[zz, yy])
    lax.fori_loop(0, 13, w_step, 0)

    def activate(rows):
        gate, up = rows[:, :F], rows[:, F:]
        hid[...] = (gate / (1.0 + jnp.exp(-gate)) * up).astype(BF16)

    def term(half, index):
        pl.when(half == 0)(lambda: activate(acc[index].reshape(128, 2 * F)))
        pl.when(half == 1)(lambda: activate(acc[:, index].reshape(128, 2 * F)))
        rows = hid[...]
        scale = coef[half, index][:, :1]
        parts = [lax.dot_general(rows, wmat[half * 4 + i, :, 2 * F:], (((1,), (1,)), ((), ())),
                                 preferred_element_type=F32) for i in range(4)]
        return jnp.concatenate(parts, axis=1) * scale

    def beside(half, sign):
        return at(mod(z + (1 - half) * sign, NZ), mod(y + half * sign, NY))

    def mine_of(half):
        return (1 - half) * z + half * y

    def rs_rows(way, part):
        start = 64 * way if part else 64 - 64 * way
        return slice(start, start + 64)

    def rs_copy(half, way, step, part):
        rows = pl.ds(rs_rows(way, part).start, 64)
        return move(rs_send.at[half, way, step, rows], rs_recv.at[half, way, step, rows],
                    rs_s.at[half, way, step, part], rs_r.at[half, way, step, part], beside(half, 1 - 2 * way))

    def begin(half, _):
        value = term(half, mod(mine_of(half) + 4, 8)).astype(BF16)
        for way in range(2):
            rs_send[half, way, 0, rs_rows(way, 1)] = value[rs_rows(way, 1)]
            rs_copy(half, way, 0, 1).start()
        return 0

    lax.fori_loop(0, 2, begin, 0)

    def go(step, _):
        def prepare(half, way):
            terms[half, way] = term(half, mod(mine_of(half) + (1 - 2 * way) * (4 - step), 8))

        def pass_on(half, part, way, first):
            rows = rs_rows(way, part)
            value = terms[half, way, rows]
            if not first:
                rs_copy(half, way, step - 1, part).wait_recv()
                value = value + rs_recv[half, way, step - 1, rows].astype(F32)
            rs_send[half, way, step, rows] = value.astype(BF16)
            rs_copy(half, way, step, part).start()

        for part in range(2):
            def each(half, _):
                for way in range(2):
                    if part == 0:
                        prepare(half, way)
                        pl.when(step == 1)(lambda: pass_on(half, part, way, True))
                        pl.when(step > 1)(lambda: pass_on(half, part, way, False))
                    else:
                        pass_on(half, part, way, False)
                return 0

            lax.fori_loop(0, 2, each, 0)
        return 0

    def fin_spread(half, there):
        mine = (1 - half) * y + half * z
        device = at((1 - half) * z + half * there, (1 - half) * there + half * y)

        @pl.when(there != mine)
        def _():
            move(fin_send.at[half, there], fin_recv.at[half, mine], fin_s.at[half], fin_r.at[half], device).start()

    def end(half, _):
        terms[half, 0] = term(half, mine_of(half))
        for part in range(2):
            rows = slice(64 * part, 64 * part + 64)
            value = terms[half, 0, rows]
            for way in range(2):
                rs_copy(half, way, 3, int(part == way)).wait_recv()
                value = value + rs_recv[half, way, 3, rows].astype(F32)
            fin_send[half, 4 * part:4 * part + 4] = value.astype(BF16).reshape(4, ROWS, HALF)
            for i in range(4):
                fin_spread(half, 4 * part + i)
        mine = (1 - half) * y + half * z
        fin_recv[half, mine] = fin_send[half, mine]
        return 0

    lax.fori_loop(1, 4, go, 0)
    lax.fori_loop(0, 2, end, 0)

    for half in range(2):
        for way in range(2):
            for step in range(3 + (way == half)):
                first(half, way, step).wait_send()
    for half in range(2):
        for way in range(2):
            rs_copy(half, way, 0, 1).wait_send()
            for step in range(1, 4):
                for part in range(2):
                    rs_copy(half, way, step, part).wait_send()

    def ring_drain(j, _):
        step = j // 4
        for half in range(2):
            for way in range(2):
                ring(half, way, step, lax.rem(j, 4) + 2 * way * (step // 3)).wait_send()
        return 0

    lax.fori_loop(0, 14, ring_drain, 0)

    def drain(g, _):
        for way in range(2):
            x_copy(g, way).wait_send()
            x_forward(g, way).wait_send()
        core_copy(g).wait_send()
        ref = wz.at[0, pl.ds(0, 7)]
        move(ref, ref, y_send.at[g], y_recv.at[g], right).wait_send()

        @pl.when(g > 0)
        def _():
            z_copy(g).wait_send()

        return 0

    lax.fori_loop(0, 8, drain, 0)

    for half in range(2):
        ref = fin_recv.at[half, pl.ds(0, 7)]
        move(ref, ref, fin_s.at[half], fin_r.at[half], right).wait_recv()
        total = fin_recv[half, 0].astype(F32)
        for i in range(1, 8):
            total = total + fin_recv[half, i].astype(F32)
        out_ref[:, half * HALF:(half + 1) * HALF] = total.astype(BF16)
        ref = fin_send.at[half, pl.ds(0, 7)]
        move(ref, ref, fin_s.at[half], fin_r.at[half], right).wait_send()


def per_device(tokens, norm_gain, expert_weights, slot_expert, pair_slots, combine_weights):
    pieces = expert_weights.reshape(NZ * NY, NX, TILES, 128).transpose(0, 2, 1, 3)
    vmem = pl.BlockSpec(memory_space=pltpu.VMEM)
    sem = pltpu.SemaphoreType.DMA
    return pl.pallas_call(
        kernel,
        out_shape=jax.ShapeDtypeStruct((ROWS, D), BF16),
        in_specs=[vmem, vmem, pl.BlockSpec(memory_space=pl.ANY), vmem, vmem, vmem],
        out_specs=vmem,
        scratch_shapes=[
            pltpu.VMEM((8, 8, ROWS, HALF), BF16),
            pltpu.VMEM((8, 8, ROWS, HALF + 128), BF16),
            pltpu.VMEM((NZ, NY, TILES, 4, 128), BF16),
            pltpu.VMEM((2, NX, NZ, NY, TILES, 4, 128), BF16),
            pltpu.VMEM((8, 256, 3 * F), BF16),
            pltpu.VMEM((8, 8, ROWS, 2 * F), F32),
            pltpu.VMEM((128, F), BF16),
            pltpu.VMEM((2, 8, 128, 128), F32),
            pltpu.VMEM((2, 2, 128, HALF), F32),
            pltpu.VMEM((2, 2, 4, 128, HALF), BF16),
            pltpu.VMEM((2, 2, 4, 128, HALF), BF16),
            pltpu.VMEM((2, 8, ROWS, HALF), BF16),
            pltpu.VMEM((2, 8, ROWS, HALF), BF16),
            sem((16,)), sem((16,)), sem((64,)), sem((64,)), sem((8,)), sem((8,)), sem((8,)), sem((8,)), sem((8,)),
            sem((2, 8)), sem((2, 8)), sem((2, 8)), sem((2, 8)), sem((8,)), sem((8,)),
            sem((2, 2, 4, 2)), sem((2, 2, 4, 2)), sem((2,)), sem((2,)),
        ],
        compiler_params=pltpu.CompilerParams(
            collective_id=0, has_side_effects=True, vmem_limit_bytes=56 * 2**20),
    )(tokens, norm_gain.reshape(1, D), pieces, slot_expert.reshape(1, 128), pair_slots.T, combine_weights.T)


def solution(mesh):
    placed = (
        P(("dp", "rep"), None),
        P(),
        P(None, ("dp", "rep"), None),
        P(),
        P(("dp", "rep"), None),
        P(("dp", "rep"), None),
    )
    return jax.shard_map(
        per_device, mesh=mesh, in_specs=placed, out_specs=P(("dp", "rep"), None), check_vma=False
    )
```

```python
import jax
import jax.numpy as jnp
from jax import lax
from jax.experimental import pallas as pl
from jax.experimental.pallas import tpu as pltpu
from jax.sharding import PartitionSpec as P

NZ, NY, NX = 8, 8, 4
D, F, ROWS = 2048, 768, 16
HALF = D // 2
TILES = 3 * F // 128
BF16, F32 = jnp.bfloat16, jnp.float32
FIRST, RING, READY, SLOTS = 0, 4, 11, 2


def mod(value, size):
    return lax.rem(value + 2 * size, size)


def kernel(tok_ref, gain_ref, w_ref, slot_ref, pair_ref, comb_ref, out_ref,
           xa, xb, wz, wraw, wmat, acc, hid, coef, terms, rs_send, rs_recv, fin_send, fin_recv,
           first_r, first_s, ring_r, ring_s, z_recv, z_send, y_recv, y_send, w_own,
           x_recv, x_send, f_recv, f_send, c_recv, c_send,
           rs_r, rs_s, fin_r, fin_s):
    dp, x = lax.axis_index("dp"), lax.axis_index("rep")
    z, y, core = dp // (2 * NY), lax.rem(dp // 2, NY), lax.rem(dp, 2)

    def at(zz, yy):
        return (zz * (2 * NY) + yy * 2 + core, x)

    def move(src, dst, send, recv, device):
        return pltpu.make_async_remote_copy(
            src_ref=src, dst_ref=dst, send_sem=send, recv_sem=recv,
            device_id=device, device_id_type=pl.DeviceIdType.MESH)

    right, left = (dp, mod(x + 1, NX)), (dp, mod(x - 1, NX))
    other = (dp + 1 - 2 * core, x)

    barrier = pltpu.get_barrier_semaphore()

    def greet(i, _):
        for device in (at(mod(z + i, NZ), y), at(z, mod(y + i, NY))):
            pl.semaphore_signal(barrier, inc=1, device_id=device, device_id_type=pl.DeviceIdType.MESH)
        return 0

    lax.fori_loop(1, 8, greet, 0)
    for device in (right, left, other):
        pl.semaphore_signal(barrier, inc=1, device_id=device, device_id_type=pl.DeviceIdType.MESH)

    acc[...] = jnp.zeros_like(acc)
    pl.semaphore_wait(barrier, 17)

    def offset(g):
        half = (g + 1) // 2
        odd = lax.rem(g, 2)
        return odd * half + (1 - odd) * lax.rem(NZ - half, NZ)

    def z_copy(g):
        zz = mod(z + offset(g), NZ)
        return move(w_ref.at[pl.ds(zz * NY, NY)], wz.at[z], z_send.at[g], z_recv.at[g], at(zz, y))

    def y_spread(g, source):
        zz = mod(z - offset(g), NZ)

        def one(i, _):
            yy = mod(y + offset(i), NY)
            move(source(zz, yy), wraw.at[core, x, zz, y], y_send.at[g], y_recv.at[g], at(z, yy)).start()
            return 0

        lax.fori_loop(1, NY, one, 0)
        pltpu.make_async_copy(source(zz, y), wraw.at[core, x, zz, y], w_own.at[g]).start()

    def y_landed(g):
        zz = mod(z - offset(g), NZ)
        ref = wraw.at[core, x, zz, pl.ds(0, 7)]
        move(ref, ref, y_send.at[g], y_recv.at[g], right).wait_recv()
        ref = wraw.at[core, x, zz, y]
        pltpu.make_async_copy(ref, ref, w_own.at[g]).wait()

    y_spread(0, lambda zz, yy: w_ref.at[zz * NY + yy])
    for g in range(1, 5):
        z_copy(g).start()

    values = tok_ref[...].astype(F32)
    mean_square = jnp.mean(values * values, axis=1, keepdims=True)
    normed = (values * lax.rsqrt(mean_square + 1e-06) * gain_ref[...]).astype(BF16)
    lane = lax.broadcasted_iota(jnp.int32, (ROWS, 128), 1)
    weights = jnp.zeros((ROWS, 128), F32)
    slots, pairs, combs = slot_ref[...].astype(F32), pair_ref[...].T, comb_ref[...].T
    for k in range(8):
        held = jnp.sum(jnp.where(lane == pairs[:, k:k + 1], slots, 0.0), axis=1, keepdims=True)
        weights = weights + jnp.where((lane & 63).astype(F32) == held, combs[:, k:k + 1], 0.0)
    high = weights.astype(BF16)
    low = (weights - high.astype(F32)).astype(BF16)
    xa[z, y] = normed[:, :HALF]
    xb[y, z, :, :HALF] = normed[:, HALF:]
    xb[y, z, :, HALF:] = jnp.where(lane < 64, high.astype(F32), low.astype(F32)).astype(BF16)

    def first(half, way, step, ahead=0):
        sign = 1 - 2 * way
        mine = (y, z)[half]
        device = at(z, mod(y + sign, NY)) if half == 0 else at(mod(z + sign, NZ), y)
        ref = (xa.at[z], xb.at[y])[half].at[mod(mine - sign * (step + ahead), 8)]
        index = (half * 2 + way) * 4 + step
        return move(ref, ref, first_s.at[index], first_r.at[index], device)

    def first_step(step):
        for half in range(2):
            for way in range(2):
                if step > 0 and (way == half or step < 4):
                    first(half, way, step - 1, 1).wait_recv()
                if step < 3 + (way == half):
                    first(half, way, step).start()

    def ring(half, way, step, part, ahead=0):
        sign = 1 - 2 * way
        mine = (z, y)[half]
        device = at(mod(z + sign, NZ), y) if half == 0 else at(z, mod(y + sign, NY))
        ref = (xa, xb)[half].at[mod(mine - sign * (step + ahead), 8), pl.ds(2 * part, 2)]
        index = ((half * 2 + way) * 4 + step) * 4 + part
        return move(ref, ref, ring_s.at[index], ring_r.at[index], device)

    def ring_landed(half, way, step, part):
        ring(half, way, step, part, 1).wait_recv()

    def rows_step(j, _):
        step = j // 4
        for half in range(2):
            for way in range(2):
                part = lax.rem(j, 4) + 2 * way * (step // 3)

                @pl.when(step > 0)
                def _(half=half, way=way, part=part):
                    ring_landed(half, way, step - 1, part)

                ring(half, way, step, part).start()
        return 0

    def rows_end():
        for half in range(2):
            for way in range(2):
                for i in range(2):
                    ring_landed(half, way, 2, 2 * (1 - way) + i)
                    ring_landed(half, way, 3, 2 * way + i)
        mine = lax.broadcasted_iota(jnp.int32, (128, 128), 1) & 63
        mine = mine == z * NY + y

        def fill(i, _):
            for half in range(2):
                raw = xb[:, i, :, HALF:] if half == 0 else xb[i, :, :, HALF:]
                c = jnp.where(mine, raw.reshape(128, 128).astype(F32), 0.0)
                coef[half, i] = jnp.broadcast_to(jnp.sum(c, axis=1, keepdims=True), (128, 128))
            return 0

        lax.fori_loop(0, 8, fill, 0)

    def place(g):
        zz = mod(z - offset(g), NZ)

        def tile(yy, _):
            for c in range(2):
                row = pl.multiple_of(yy * 32 + c * 16, 16)
                for t in range(TILES):
                    wmat[zz, pl.ds(row, 16), t * 128:(t + 1) * 128] = jnp.concatenate(
                        [wraw[c, i, zz, yy, t] for i in range(NX)], axis=0)
            return 0

        lax.fori_loop(0, NY, tile, 0)

    def multiply(g, _):
        zz = mod(z - offset(g), NZ)

        def add(rows_of, first):
            column = pl.multiple_of((zz - first) * 256, 256)

            rows = rows_of(column)
            for n in range(3):
                at_n = slice(n * 512, (n + 1) * 512)
                part_of = jnp.dot(rows, wmat[zz, :, at_n], preferred_element_type=F32)
                acc[:, :, :, at_n] += part_of.reshape(8, 8, ROWS, 512)

        @pl.when(zz < 4)
        def _():
            add(lambda col: xa[:, :, :, pl.ds(col, 256)].reshape(1024, 256), 0)

        @pl.when(zz >= 4)
        def _():
            add(lambda col: jnp.concatenate(
                [xb[:, i, :, pl.ds(col, 256)].reshape(128, 256) for i in range(8)], axis=0), 4)

        return 0

    def x_copy(g, way):
        zz = mod(z - offset(g), NZ)
        ref = wraw.at[core, x, zz]
        return move(ref, ref, x_send.at[way, g], x_recv.at[way, g], (right, left)[way])

    def x_forward(g, way):
        zz = mod(z - offset(g), NZ)
        ref = wraw.at[core, mod(x - 1 + 2 * way, NX), zz, pl.ds(4 * way, 4)]
        return move(ref, ref, f_send.at[way, g], f_recv.at[way, g], (right, left)[way])

    def core_copy(g):
        zz = mod(z - offset(g), NZ)
        ref = wraw.at[core, :, zz]
        return move(ref, ref, c_send.at[g], c_recv.at[g], other)

    def w_step(s, _):
        @pl.when(s < 3)
        def _():
            z_copy(s + 5).start()

        @pl.when(s < 6)
        def _():
            z_copy(s + 2).wait_recv()
            y_spread(s + 2, lambda zz, yy: wz.at[zz, yy])

        @pl.when(s < 8)
        def _():
            y_landed(s)
            for way in range(2):
                x_copy(s, way).start()

        for i in range(5):
            pl.when(s == FIRST + i)(lambda i=i: first_step(i))

        @pl.when((s >= RING) & (s < READY))
        def _():
            lax.fori_loop(SLOTS * (s - RING), jnp.minimum(SLOTS * (s - RING + 1), 14), rows_step, 0)

        pl.when(s == READY)(rows_end)

        @pl.when((s >= 1) & (s < 9))
        def _():
            for way in range(2):
                x_copy(s - 1, way).wait_recv()
                x_forward(s - 1, way).start()

        @pl.when((s >= 3) & (s < 11))
        def _():
            for way in range(2):
                x_forward(s - 3, way).wait_recv()
            core_copy(s - 3).start()

        @pl.when(s >= 4)
        def _():
            core_copy(s - 4).wait_recv()
            place(s - 4)

        @pl.when(s == READY)
        def _():
            lax.fori_loop(0, READY - 3, multiply, 0)

        return 0

    z_copy(1).wait_recv()
    y_spread(1, lambda zz, yy: wz.at[zz, yy])
    lax.fori_loop(0, 12, w_step, 0)

    def activate(rows):
        gate, up = rows[:, :F], rows[:, F:]
        hid[...] = (gate / (1.0 + jnp.exp(-gate)) * up).astype(BF16)

    def term(half, index):
        pl.when(half == 0)(lambda: activate(acc[index].reshape(128, 2 * F)))
        pl.when(half == 1)(lambda: activate(acc[:, index].reshape(128, 2 * F)))
        rows = hid[...]
        scale = coef[half, index][:, :1]
        parts = [lax.dot_general(rows, wmat[half * 4 + i, :, 2 * F:], (((1,), (1,)), ((), ())),
                                 preferred_element_type=F32) for i in range(4)]
        return jnp.concatenate(parts, axis=1) * scale

    def beside(half, sign):
        return at(mod(z + (1 - half) * sign, NZ), mod(y + half * sign, NY))

    def mine_of(half):
        return (1 - half) * z + half * y

    def rs_rows(way, part):
        start = 64 * way if part else 64 - 64 * way
        return slice(start, start + 64)

    def rs_copy(half, way, step, part):
        rows = pl.ds(rs_rows(way, part).start, 64)
        return move(rs_send.at[half, way, step, rows], rs_recv.at[half, way, step, rows],
                    rs_s.at[half, way, step, part], rs_r.at[half, way, step, part], beside(half, 1 - 2 * way))

    def begin(half, _):
        value = term(half, mod(mine_of(half) + 4, 8)).astype(BF16)
        for way in range(2):
            rs_send[half, way, 0, rs_rows(way, 1)] = value[rs_rows(way, 1)]
            rs_copy(half, way, 0, 1).start()
        return 0

    lax.fori_loop(0, 2, begin, 0)

    def go(step, _):
        def prepare(half, way):
            terms[half, way] = term(half, mod(mine_of(half) + (1 - 2 * way) * (4 - step), 8))

        def pass_on(half, part, way, first):
            rows = rs_rows(way, part)
            value = terms[half, way, rows]
            if not first:
                rs_copy(half, way, step - 1, part).wait_recv()
                value = value + rs_recv[half, way, step - 1, rows].astype(F32)
            rs_send[half, way, step, rows] = value.astype(BF16)
            rs_copy(half, way, step, part).start()

        for part in range(2):
            def each(half, _):
                for way in range(2):
                    if part == 0:
                        prepare(half, way)
                        pl.when(step == 1)(lambda: pass_on(half, part, way, True))
                        pl.when(step > 1)(lambda: pass_on(half, part, way, False))
                    else:
                        pass_on(half, part, way, False)
                return 0

            lax.fori_loop(0, 2, each, 0)
        return 0

    def fin_spread(half, there):
        mine = (1 - half) * y + half * z
        device = at((1 - half) * z + half * there, (1 - half) * there + half * y)

        @pl.when(there != mine)
        def _():
            move(fin_send.at[half, there], fin_recv.at[half, mine], fin_s.at[half], fin_r.at[half], device).start()

    def end(half, _):
        terms[half, 0] = term(half, mine_of(half))
        for part in range(2):
            rows = slice(64 * part, 64 * part + 64)
            value = terms[half, 0, rows]
            for way in range(2):
                rs_copy(half, way, 3, int(part == way)).wait_recv()
                value = value + rs_recv[half, way, 3, rows].astype(F32)
            fin_send[half, 4 * part:4 * part + 4] = value.astype(BF16).reshape(4, ROWS, HALF)
            for i in range(4):
                fin_spread(half, 4 * part + i)
        mine = (1 - half) * y + half * z
        fin_recv[half, mine] = fin_send[half, mine]
        return 0

    lax.fori_loop(1, 4, go, 0)
    lax.fori_loop(0, 2, end, 0)

    for half in range(2):
        for way in range(2):
            for step in range(3 + (way == half)):
                first(half, way, step).wait_send()
    for half in range(2):
        for way in range(2):
            rs_copy(half, way, 0, 1).wait_send()
            for step in range(1, 4):
                for part in range(2):
                    rs_copy(half, way, step, part).wait_send()

    def ring_drain(j, _):
        step = j // 4
        for half in range(2):
            for way in range(2):
                ring(half, way, step, lax.rem(j, 4) + 2 * way * (step // 3)).wait_send()
        return 0

    lax.fori_loop(0, 14, ring_drain, 0)

    def drain(g, _):
        for way in range(2):
            x_copy(g, way).wait_send()
            x_forward(g, way).wait_send()
        core_copy(g).wait_send()
        ref = wz.at[0, pl.ds(0, 7)]
        move(ref, ref, y_send.at[g], y_recv.at[g], right).wait_send()

        @pl.when(g > 0)
        def _():
            z_copy(g).wait_send()

        return 0

    lax.fori_loop(0, 8, drain, 0)

    for half in range(2):
        ref = fin_recv.at[half, pl.ds(0, 7)]
        move(ref, ref, fin_s.at[half], fin_r.at[half], right).wait_recv()
        total = fin_recv[half, 0].astype(F32)
        for i in range(1, 8):
            total = total + fin_recv[half, i].astype(F32)
        out_ref[:, half * HALF:(half + 1) * HALF] = total.astype(BF16)
        ref = fin_send.at[half, pl.ds(0, 7)]
        move(ref, ref, fin_s.at[half], fin_r.at[half], right).wait_send()


def per_device(tokens, norm_gain, expert_weights, slot_expert, pair_slots, combine_weights):
    pieces = expert_weights.reshape(NZ * NY, NX, TILES, 128).transpose(0, 2, 1, 3)
    vmem = pl.BlockSpec(memory_space=pltpu.VMEM)
    sem = pltpu.SemaphoreType.DMA
    return pl.pallas_call(
        kernel,
        out_shape=jax.ShapeDtypeStruct((ROWS, D), BF16),
        in_specs=[vmem, vmem, pl.BlockSpec(memory_space=pl.ANY), vmem, vmem, vmem],
        out_specs=vmem,
        scratch_shapes=[
            pltpu.VMEM((8, 8, ROWS, HALF), BF16),
            pltpu.VMEM((8, 8, ROWS, HALF + 128), BF16),
            pltpu.VMEM((NZ, NY, TILES, 4, 128), BF16),
            pltpu.VMEM((2, NX, NZ, NY, TILES, 4, 128), BF16),
            pltpu.VMEM((8, 256, 3 * F), BF16),
            pltpu.VMEM((8, 8, ROWS, 2 * F), F32),
            pltpu.VMEM((128, F), BF16),
            pltpu.VMEM((2, 8, 128, 128), F32),
            pltpu.VMEM((2, 2, 128, HALF), F32),
            pltpu.VMEM((2, 2, 4, 128, HALF), BF16),
            pltpu.VMEM((2, 2, 4, 128, HALF), BF16),
            pltpu.VMEM((2, 8, ROWS, HALF), BF16),
            pltpu.VMEM((2, 8, ROWS, HALF), BF16),
            sem((16,)), sem((16,)), sem((64,)), sem((64,)), sem((8,)), sem((8,)), sem((8,)), sem((8,)), sem((8,)),
            sem((2, 8)), sem((2, 8)), sem((2, 8)), sem((2, 8)), sem((8,)), sem((8,)),
            sem((2, 2, 4, 2)), sem((2, 2, 4, 2)), sem((2,)), sem((2,)),
        ],
        compiler_params=pltpu.CompilerParams(
            collective_id=0, has_side_effects=True, vmem_limit_bytes=56 * 2**20),
    )(tokens, norm_gain.reshape(1, D), pieces, slot_expert.reshape(1, 128), pair_slots.T, combine_weights.T)


def solution(mesh):
    placed = (
        P(("dp", "rep"), None),
        P(),
        P(None, ("dp", "rep"), None),
        P(),
        P(("dp", "rep"), None),
        P(("dp", "rep"), None),
    )
    return jax.shard_map(
        per_device, mesh=mesh, in_specs=placed, out_specs=P(("dp", "rep"), None), check_vma=False
    )
```
